32 devices in a mesh: grp: 2 (over x), src: 8 (over z, y), tgt: 2 (over core).
Axes of the slice: x: 2, y: 2, z: 4, core: 2. Of those that a mesh axis runs over, the one named last changes fastest.
Arguments:
- src_points: bfloat16 [4096, 64], P(('grp', 'src')), parts along dimension 0
- tgt_points: bfloat16 [65536, 64], P(('grp', 'tgt')), parts along dimension 0
- src_logw: float32 [4096], P(('grp', 'src')), parts along dimension 0, may hold values from -1 to 1
- tgt_logw: float32 [65536], P(('grp', 'tgt')), parts along dimension 0, may hold values from -1 to 1
- src_count: int32 [32], P(('grp', 'src')), parts along dimension 0, may hold values from 1 to 128, as said below
- tgt_count: int32 [512], P(('grp', 'tgt')), parts along dimension 0, may hold values from 1 to 128, as said below
- kept: int32 [32, 256], P(('grp', 'src'), 'tgt'), parts along dimension 0, may hold values from 0 to 1, as said below
- g_init: float32 [65536], P(('grp', 'tgt')), parts along dimension 0, may hold values from -4 to 4
Outputs:
- src_potential: float32 [4096], P(('grp', 'src')), parts along dimension 0
- tgt_potential: float32 [65536], P(('grp', 'tgt')), parts along dimension 0
The draws below stay inside these ranges and needn't reach their ends.
There are 2 independent parts, one for each index of `grp`. The reference program is written for one: setup_inputs(seed, part) draws one part's arguments, and reference() takes and returns one part's arrays. A program takes and returns all parts, laid end to end along the dimension named above; each array names one. Nothing has to cross between parts.
Inputs may be any that keep to these rules, and one draw needn't show every extreme that they name: Every source cluster and every target cluster has at least one kept block. `src_count`: some source cluster is full. `tgt_count`: some target cluster is full.
All inputs are finite; a program needn't handle non-finite values.
Results may differ from the reference program's by a relative error of at most 0.0003.
Values sent between devices are 32-bit elements; how exact they have to be, the bound alone decides.
A program may use at most 128 MiB of HBM per device.

```python
import jax
import jax.numpy as jnp
from jax import lax

DIM = 64
CL = 128
ITERS = 2
SC = 16
TC = 256
NS = 2048
NT = 32768


def partners(key):
    link_key = jax.random.fold_in(key, 77)
    src_partner = jax.random.randint(jax.random.fold_in(link_key, 1), (SC,), 0, TC)
    tgt_partner = jax.random.randint(jax.random.fold_in(link_key, 2), (TC,), 0, SC)
    return (src_partner, tgt_partner)


def target_pool(key):
    pool_key = jax.random.fold_in(key, 91)
    gaussian = jax.random.normal(jax.random.fold_in(pool_key, 1), (NT, DIM), jnp.float32)
    return gaussian


def draw_kept(key, part):
    src_partner, tgt_partner = partners(key)
    key = jax.random.fold_in(key, 3)
    density = jax.random.randint(jax.random.fold_in(key, 1), (SC, 1), 5, 400)
    ticket = jax.random.randint(jax.random.fold_in(key, 2), (SC, TC), 0, 1000)
    row_index = jnp.arange(SC, dtype=jnp.int32)[:, None]
    col_index = jnp.arange(TC, dtype=jnp.int32)[None, :]
    linked = (ticket < density) | (col_index == src_partner[:, None]) | (row_index == tgt_partner[None, :])
    return linked.astype(jnp.int32)


def draw_tgt_points(key, part):
    gaussian = target_pool(key)
    return (gaussian * 0.25).astype(jnp.bfloat16)


def draw_src_points(key, part):
    key = jax.random.fold_in(key, 5)
    return (jax.random.normal(jax.random.fold_in(key, 3), (NS, DIM), jnp.float32) * 0.25).astype(jnp.bfloat16)


def draw_counts(key, clusters):
    sizes = jax.random.randint(jax.random.fold_in(key, 1), (clusters,), 1, CL + 1)
    widest = jax.random.randint(jax.random.fold_in(key, 2), (), 0, clusters)
    return sizes.at[widest].set(CL)


def draw_src_count(key, part):
    key = jax.random.fold_in(key, 6)
    return draw_counts(key, SC)


def draw_tgt_count(key, part):
    key = jax.random.fold_in(key, 7)
    return draw_counts(key, TC)


def steps_of(own_key, dims, pieces, smallest, high):
    loudness = 1.0
    for position, blocks in pieces:
        heights = jax.random.uniform(jax.random.fold_in(jax.random.fold_in(own_key, 6), position), (blocks,), jnp.float32, smallest / len(pieces), high / len(pieces))
        loudness = loudness * jnp.repeat(jnp.exp(heights), dims[position] // blocks).reshape((-1,) + (1,) * (len(dims) - 1 - position))
    return loudness


def noise(stream_key, dims, scale, reach, cuts=(), kind=jnp.bfloat16):
    array = jax.random.normal(stream_key, dims, jnp.float32) * scale
    if len(cuts) > 0:
        array = steps_of(stream_key, dims, cuts, -0.22, 0.18) * array
    return jnp.clip(array, min=-reach, max=reach).astype(kind)


def setup_inputs(seed: int = 0, part: int = 0) -> dict:
    key_of = jax.random.split(jax.random.key(seed), 9)
    part_splits = jax.random.split(jax.random.fold_in(key_of[8], part), 9)
    src_points = draw_src_points(jax.random.fold_in(jax.random.fold_in(key_of[8], part), 71), part)
    tgt_points = draw_tgt_points(jax.random.fold_in(jax.random.fold_in(key_of[8], part), 71), part)
    src_logw = jnp.clip(jax.random.uniform(part_splits[2], (NS,), jnp.float32, -1.0, 1.0) * steps_of(part_splits[2], (NS,), ((0, 8),), -0.4, 0.0), -1.0, 1.0)
    tgt_logw = jnp.clip(jax.random.uniform(part_splits[3], (NT,), jnp.float32, -1.0, 1.0) * steps_of(part_splits[3], (NT,), ((0, 2),), -0.4, 0.0), -1.0, 1.0)
    src_count = draw_src_count(jax.random.fold_in(jax.random.fold_in(key_of[8], part), 71), part)
    tgt_count = draw_tgt_count(jax.random.fold_in(jax.random.fold_in(key_of[8], part), 71), part)
    kept = draw_kept(jax.random.fold_in(jax.random.fold_in(key_of[8], part), 71), part)
    g_init = noise(part_splits[7], (NT,), 1.0, 4.0, ((0, 2),), jnp.float32)
    return dict(src_points=src_points, tgt_points=tgt_points, src_logw=src_logw, tgt_logw=tgt_logw, src_count=src_count, tgt_count=tgt_count, kept=kept, g_init=g_init)


EPS = 0.25
NEG = -1.0e30


def expand_clusters(cluster_flags, row_count, col_count):
    count_a, count_b = cluster_flags.shape
    broadcast_flags = jnp.broadcast_to(cluster_flags[:, None, :, None], (count_a, row_count, count_b, col_count))
    return broadcast_flags.reshape(count_a * row_count, count_b * col_count)


def valid_points(counts):
    positions = jnp.arange(CL, dtype=jnp.int32)
    return (positions[None, :] < counts[:, None]).reshape(-1)


def half_norm(points):
    values = points.astype(jnp.float32)
    return 0.5 * jnp.sum(values * values, axis=1)


def soft_min(own_points, own_norm, cluster_flags, other_points, other_norm, other_valid, other_logw, other_pot):
    products = jnp.dot(own_points, other_points.T, preferred_element_type=jnp.float32)
    cost_tile = own_norm[:, None] + other_norm[None, :] - products
    allowed = expand_clusters(cluster_flags[None, :], CL, CL) & other_valid[None, :]
    scores = jnp.where(allowed, other_logw[None, :] + (other_pot[None, :] - cost_tile) / EPS, NEG)
    row_top = jnp.max(scores, axis=1)
    exp_total = jnp.sum(jnp.where(allowed, jnp.exp(scores - row_top[:, None]), 0.0), axis=1)
    return -EPS * (row_top + jnp.log(exp_total))


def reference(src_points, tgt_points, src_logw, tgt_logw, src_count, tgt_count, kept, g_init):
    src_norm = half_norm(src_points)
    tgt_norm = half_norm(tgt_points)
    src_valid = valid_points(src_count)
    tgt_valid = valid_points(tgt_count)
    flag_table = kept > 0
    src_groups = (src_points.reshape(-1, CL, DIM), src_norm.reshape(-1, CL), flag_table)
    tgt_groups = (tgt_points.reshape(-1, CL, DIM), tgt_norm.reshape(-1, CL), flag_table.T)
    tgt_pot = g_init
    src_pot = jnp.zeros(src_norm.shape, jnp.float32)
    for rounds in range(ITERS):
        current_tgt = tgt_pot
        src_pot = lax.map(lambda cluster_group: soft_min(cluster_group[0], cluster_group[1], cluster_group[2], tgt_points, tgt_norm, tgt_valid, tgt_logw, current_tgt), src_groups).reshape(-1)
        current_src = src_pot
        tgt_pot = lax.map(lambda cluster_group: soft_min(cluster_group[0], cluster_group[1], cluster_group[2], src_points, src_norm, src_valid, src_logw, current_src), tgt_groups).reshape(-1)
    return (src_pot, tgt_pot)
```

```python
import functools
import math

import jax
import jax.numpy as jnp
from jax import lax
from jax.experimental import pallas as pl
from jax.experimental.pallas import tpu as pltpu
from jax.sharding import PartitionSpec as P

ITERS = 2
EPS = 0.25
NEG = -1e30
LOG2E = math.log2(math.e)
SCALE = LOG2E / EPS
MESH = pl.DeviceIdType.MESH


def log_two(x):
    return jnp.log(x) * LOG2E


def tree(op, terms):
    terms = list(terms)
    while len(terms) > 1:
        joined = [op(a, b) for a, b in zip(terms[::2], terms[1::2])]
        terms = joined + terms[len(terms) & ~1 :]
    return terms[0]


def kernel(
    dims,
    xt_ref,
    yt_ref,
    src_logw_ref,
    tgt_logw_ref,
    src_count_ref,
    tgt_count_ref,
    kept_ref,
    g_init_ref,
    out_src_ref,
    out_tgt_ref,
    x_ref,
    prod_ref,
    base_ref,
    mask_ref,
    norm_ref,
    top_ref,
    sum_ref,
    bias_ref,
    col_top_ref,
    col_sum_ref,
    row_buf,
    part_buf,
    recv_buf,
    pot_buf,
    row_send,
    row_recv,
    part_send,
    part_recv,
    pot_send,
    pot_recv,
):
    clusters, tiles, width, peers, halves, groups, size = dims
    rows = clusters * width
    me = lax.axis_index("src")
    my_half = lax.axis_index("tgt")

    barrier = pltpu.get_barrier_semaphore()

    def greet(step, carry):
        peer = lax.rem(me + step, peers)
        pl.semaphore_signal(barrier, inc=1, device_id={"src": peer}, device_id_type=MESH)
        return carry

    lax.fori_loop(1, peers, greet, 0)
    for step in range(1, halves):
        other = lax.rem(my_half + step, halves)
        pl.semaphore_signal(barrier, inc=1, device_id={"tgt": other}, device_id_type=MESH)

    def row_copy(rounds, slot, other):
        return pltpu.make_async_remote_copy(
            src_ref=row_buf.at[rounds, slot],
            dst_ref=row_buf.at[rounds, slot],
            send_sem=row_send.at[rounds, other],
            recv_sem=row_recv.at[rounds, slot],
            device_id={"tgt": other},
            device_id_type=MESH,
        )

    def part_copy(rounds, slot, peer):
        return pltpu.make_async_remote_copy(
            src_ref=part_buf.at[rounds, peer],
            dst_ref=recv_buf.at[rounds, slot],
            send_sem=part_send.at[rounds, peer],
            recv_sem=part_recv.at[rounds, slot],
            device_id={"src": peer},
            device_id_type=MESH,
        )

    def pot_copy(rounds, slot, peer):
        return pltpu.make_async_remote_copy(
            src_ref=pot_buf.at[rounds, slot],
            dst_ref=pot_buf.at[rounds, slot],
            send_sem=pot_send.at[rounds, peer],
            recv_sem=pot_recv.at[rounds, slot],
            device_id={"src": peer},
            device_id_type=MESH,
        )

    line = lax.broadcasted_iota(jnp.int32, (width, width), 1)
    eye = lax.broadcasted_iota(jnp.int32, (width, width), 0) == line
    square = lax.broadcasted_iota(jnp.int32, (tiles, width), 1)
    across = lax.broadcasted_iota(jnp.int32, (tiles, tiles), 1)
    tile_eye = lax.broadcasted_iota(jnp.int32, (tiles, tiles), 0) == across

    def column(row, diagonal):
        spread = jnp.broadcast_to(row, diagonal.shape)
        return jnp.sum(jnp.where(diagonal, spread, 0.0), axis=1, keepdims=True)

    xt = xt_ref[...].astype(jnp.float32)
    src_norm = 0.5 * jnp.sum(xt * xt, axis=0, keepdims=True)
    x_ref[...] = xt.T.astype(x_ref.dtype)

    tgt_count = column(tgt_count_ref[...].astype(jnp.float32), tile_eye)
    tgt_valid = square.astype(jnp.float32) < tgt_count
    logw = jnp.where(tgt_valid, tgt_logw_ref[...] * LOG2E, NEG)
    for a in range(clusters):
        flags = column(kept_ref[a : a + 1, :].astype(jnp.float32), tile_eye)
        closed = jnp.broadcast_to(jnp.where(flags > 0.5, 0.0, NEG), (tiles, width))
        base = logw + closed
        for p in range(peers):
            for h in range(groups):
                first = (p * groups + h) * size
                mask_ref[a, p, h] = closed[first : first + size]
                base_ref[a, p, h] = base[first : first + size]
    top_ref[...] = jnp.full(top_ref.shape, NEG, jnp.float32)
    sum_ref[...] = jnp.zeros(sum_ref.shape, jnp.float32)

    block = 16

    def absorb(p, h, potential, products):
        for a in range(clusters):
            added = base_ref[a, p, h] + potential
            for first in range(a * width, (a + 1) * width, block):
                scores = [
                    products(k, first) + jnp.broadcast_to(added[k : k + 1], (block, width))
                    for k in range(size)
                ]
                at = pl.ds(first, block)
                old = top_ref[at, :]
                top = jnp.maximum(old, tree(jnp.maximum, scores))
                total = tree(jnp.add, [jnp.exp2(score - top) for score in scores])
                sum_ref[at, :] = sum_ref[at, :] * jnp.exp2(old - top) + total
                top_ref[at, :] = top

    def first_rows(q, carry):
        p, h = q // groups, lax.rem(q, groups)
        start = pl.multiple_of(q * (size * width), size * width)
        yt = yt_ref[:, pl.ds(start, size * width)]
        values = yt.astype(jnp.float32)
        norm = 0.5 * jnp.sum(values * values, axis=0, keepdims=True)
        for k in range(size):
            norm_ref[p, h, k : k + 1, :] = norm[:, k * width : (k + 1) * width]
        dots = SCALE * lax.dot_general(
            x_ref[...], yt, (((1,), (0,)), ((), ())), preferred_element_type=jnp.float32
        )
        for k in range(size):
            prod_ref[q * size + k] = dots[:, k * width : (k + 1) * width]

        def products(k, first):
            return dots[first : first + block, k * width : (k + 1) * width]

        absorb(p, h, SCALE * (g_init_ref[p, h] - norm_ref[p, h]), products)
        return carry

    def later_rows(rounds, p):
        for h in range(groups):

            def products(k, first):
                return prod_ref[(p * groups + h) * size + k, pl.ds(first, block), :]

            absorb(p, h, pot_buf[rounds - 1, p, h], products)

    def columns(p, h):
        for k in range(size):
            tile = (p * groups + h) * size + k
            for a in range(clusters):
                scores = [
                    prod_ref[tile, pl.ds(first, 8), :] + bias_ref[pl.ds(first, 8), :]
                    for first in range(a * width, (a + 1) * width, 8)
                ]
                top = tree(jnp.maximum, scores)
                total = tree(jnp.add, [jnp.exp2(score - top) for score in scores])
                best = jnp.max(top, axis=0, keepdims=True)
                total = jnp.sum(total * jnp.exp2(top - best), axis=0, keepdims=True)
                col_top_ref[h, a, k : k + 1, :] = best
                col_sum_ref[h, a, k : k + 1, :] = total
        tops = [col_top_ref[h, a] + mask_ref[a, p, h] for a in range(clusters)]
        best = tree(jnp.maximum, tops)
        total = tree(
            jnp.add, [col_sum_ref[h, a] * jnp.exp2(tops[a] - best) for a in range(clusters)]
        )
        return best + log_two(total)

    for rounds in range(ITERS):
        if rounds == 0:
            lax.fori_loop(0, peers * groups, first_rows, 0)
            pl.semaphore_wait(barrier, peers - 1 + halves - 1)
        else:
            top_ref[...] = jnp.full(top_ref.shape, NEG, jnp.float32)
            sum_ref[...] = jnp.zeros(sum_ref.shape, jnp.float32)
            later_rows(rounds, me)

            def arrived(step, carry, rounds=rounds):
                p = lax.rem(me + step, peers)
                pot_copy(rounds - 1, p, p).wait_recv()
                later_rows(rounds, p)
                return carry

            lax.fori_loop(1, peers, arrived, 0)

        top = top_ref[...]
        best = jnp.max(top, axis=1, keepdims=True)
        total = jnp.sum(sum_ref[...] * jnp.exp2(top - best), axis=1, keepdims=True)
        level = jnp.broadcast_to(best + log_two(total), (rows, width))
        for a in range(clusters):
            own = jnp.where(eye, level[a * width : (a + 1) * width], 0.0)
            row_buf[rounds, my_half, a : a + 1, :] = jnp.sum(own, axis=0, keepdims=True)
        others = [lax.rem(my_half + step, halves) for step in range(1, halves)]
        for other in others:
            row_copy(rounds, my_half, other).start()
        for other in others:
            row_copy(rounds, other, other).wait_recv()
        levels = [row_buf[rounds, half] for half in range(halves)]
        best = tree(jnp.maximum, levels)
        total = tree(jnp.add, [jnp.exp2(level - best) for level in levels])
        src_pot = -(best + log_two(total))
        for a in range(clusters):
            live = line[:1] < src_count_ref[a]
            own = src_logw_ref[a : a + 1, :] * LOG2E + src_pot[a : a + 1]
            bias = column(jnp.where(live, own, NEG), eye)
            bias_ref[a * width : (a + 1) * width, :] = jnp.broadcast_to(bias, (width, width))

        def send_part(step, carry, rounds=rounds):
            p = lax.rem(me + step, peers)
            for h in range(groups):
                part_buf[rounds, p, h] = columns(p, h)
            part_copy(rounds, me, p).start()
            return carry

        lax.fori_loop(1, peers, send_part, 0)
        for h in range(groups):
            recv_buf[rounds, me, h] = columns(me, h)

        def got_part(step, carry, rounds=rounds):
            p = lax.rem(me + step, peers)
            part_copy(rounds, p, p).wait_recv()
            return carry

        lax.fori_loop(1, peers, got_part, 0)
        levels = [recv_buf[rounds, p] for p in range(peers)]
        best = tree(jnp.maximum, levels)
        total = tree(jnp.add, [jnp.exp2(level - best) for level in levels])
        tgt_pot = -(best + log_two(total))
        if rounds == ITERS - 1:
            tgt_pot = tgt_pot * (1.0 / SCALE) + norm_ref[me]
        pot_buf[rounds, me] = tgt_pot

        def send_pot(step, carry, rounds=rounds):
            pot_copy(rounds, me, lax.rem(me + step, peers)).start()
            return carry

        lax.fori_loop(1, peers, send_pot, 0)

    for a in range(clusters):
        norm = src_norm[:, a * width : (a + 1) * width]
        out_src_ref[a : a + 1, :] = src_pot[a : a + 1] * (1.0 / SCALE) + norm

    def got_pot(step, carry):
        p = lax.rem(me + step, peers)
        pot_copy(ITERS - 1, p, p).wait_recv()
        return carry

    lax.fori_loop(1, peers, got_pot, 0)
    out_tgt_ref[...] = pot_buf[ITERS - 1]

    for rounds in range(ITERS):
        for other in others:
            row_copy(rounds, my_half, other).wait_send()

        def sent(step, carry, rounds=rounds):
            p = lax.rem(me + step, peers)
            part_copy(rounds, me, p).wait_send()
            pot_copy(rounds, me, p).wait_send()
            return carry

        lax.fori_loop(1, peers, sent, 0)


def local(src_points, tgt_points, src_logw, tgt_logw, src_count, tgt_count, kept, g_init):
    rows, feature = src_points.shape
    tgt_rows = tgt_points.shape[0]
    clusters = src_count.shape[0]
    tiles = tgt_count.shape[0]
    width = rows // clusters
    peers = lax.axis_size("src")
    halves = lax.axis_size("tgt")
    share = tiles // peers
    size = math.gcd(share, 8)
    groups = share // size
    dims = (clusters, tiles, width, peers, halves, groups, size)
    cut = (peers, groups, size, width)
    f32 = jnp.float32
    vmem = pl.BlockSpec(memory_space=pltpu.VMEM)
    smem = pl.BlockSpec(memory_space=pltpu.SMEM)
    dma = pltpu.SemaphoreType.DMA
    src_pot, tgt_pot = pl.pallas_call(
        functools.partial(kernel, dims),
        out_shape=(jax.ShapeDtypeStruct((clusters, width), f32), jax.ShapeDtypeStruct(cut, f32)),
        in_specs=[vmem, vmem, vmem, vmem, smem, vmem, vmem, vmem],
        out_specs=(vmem, vmem),
        scratch_shapes=[
            pltpu.VMEM((rows, feature), src_points.dtype),
            pltpu.VMEM((tiles, rows, width), f32),
            pltpu.VMEM((clusters,) + cut, f32),
            pltpu.VMEM((clusters,) + cut, f32),
            pltpu.VMEM(cut, f32),
            pltpu.VMEM((rows, width), f32),
            pltpu.VMEM((rows, width), f32),
            pltpu.VMEM((rows, width), f32),
            pltpu.VMEM((groups, clusters, size, width), f32),
            pltpu.VMEM((groups, clusters, size, width), f32),
            pltpu.VMEM((ITERS, halves, clusters, width), f32),
            pltpu.VMEM((ITERS,) + cut, f32),
            pltpu.VMEM((ITERS,) + cut, f32),
            pltpu.VMEM((ITERS,) + cut, f32),
            dma((ITERS, halves)),
            dma((ITERS, halves)),
            dma((ITERS, peers)),
            dma((ITERS, peers)),
            dma((ITERS, peers)),
            dma((ITERS, peers)),
        ],
        compiler_params=pltpu.CompilerParams(
            collective_id=0, has_side_effects=True, vmem_limit_bytes=40 * 1024 * 1024
        ),
    )(
        src_points.T,
        tgt_points.T,
        src_logw.reshape(clusters, width),
        tgt_logw.reshape(tiles, width),
        src_count,
        tgt_count.reshape(1, tiles),
        kept,
        g_init.reshape(cut),
    )
    return (src_pot.reshape(rows), tgt_pot.reshape(tgt_rows))


def solution(mesh):
    return jax.shard_map(
        local,
        mesh=mesh,
        in_specs=(
            P(("grp", "src"), None),
            P(("grp", "tgt"), None),
            P(("grp", "src")),
            P(("grp", "tgt")),
            P(("grp", "src")),
            P(("grp", "tgt")),
            P(("grp", "src"), "tgt"),
            P(("grp", "tgt")),
        ),
        out_specs=(P(("grp", "src")), P(("grp", "tgt"))),
        check_vma=False,
    )
```

```python
import functools
import math

import jax
import jax.numpy as jnp
from jax import lax
from jax.experimental import pallas as pl
from jax.experimental.pallas import tpu as pltpu
from jax.sharding import PartitionSpec as P

ITERS = 2
EPS = 0.25
NEG = -1e30
LOG2E = math.log2(math.e)
SCALE = LOG2E / EPS
MESH = pl.DeviceIdType.MESH


def log_two(x):
    return jnp.log(x) * LOG2E


def tree(op, terms):
    terms = list(terms)
    while len(terms) > 1:
        joined = [op(a, b) for a, b in zip(terms[::2], terms[1::2])]
        terms = joined + terms[len(terms) & ~1 :]
    return terms[0]


def kernel(
    dims,
    xt_hbm,
    yt_hbm,
    src_logw_hbm,
    tgt_logw_hbm,
    src_count_hbm,
    tgt_count_hbm,
    kept_hbm,
    g_init_hbm,
    out_src_ref,
    out_tgt_ref,
    xt_ref,
    yt_ref,
    src_logw_ref,
    tgt_logw_ref,
    src_count_ref,
    tgt_count_ref,
    kept_ref,
    g_init_ref,
    load_sems,
    yt_sems,
    x_ref,
    prod_ref,
    base_ref,
    mask_ref,
    norm_ref,
    top_ref,
    sum_ref,
    bias_ref,
    col_top_ref,
    col_sum_ref,
    row_buf,
    part_buf,
    recv_buf,
    pot_buf,
    row_send,
    row_recv,
    part_send,
    part_recv,
    pot_send,
    pot_recv,
):
    clusters, tiles, width, peers, halves, groups, size = dims
    rows = clusters * width
    me = lax.axis_index("src")
    my_half = lax.axis_index("tgt")

    loads = [
        pltpu.make_async_copy(here, there, load_sems.at[place])
        for place, (here, there) in enumerate(
            (
                (tgt_count_hbm, tgt_count_ref),
                (kept_hbm, kept_ref),
                (tgt_logw_hbm, tgt_logw_ref),
                (xt_hbm, xt_ref),
                (g_init_hbm, g_init_ref),
                (src_logw_hbm, src_logw_ref),
                (src_count_hbm, src_count_ref),
            )
        )
    ]
    for load in loads:
        load.start()
    span = size * width

    def load_targets(q):
        at = pl.ds(pl.multiple_of(q * span, span), span)
        return pltpu.make_async_copy(yt_hbm.at[:, at], yt_ref.at[:, at], yt_sems.at[q])

    def start_targets(q, carry):
        load_targets(q).start()
        return carry

    lax.fori_loop(0, peers * groups, start_targets, 0)

    def partner(step):
        if peers & (peers - 1):
            return lax.rem(me + step, peers)
        found, bit = 0, 1
        while bit < peers:
            found = found + lax.rem(me // bit + step // bit, 2) * bit
            bit *= 2
        return found

    barrier = pltpu.get_barrier_semaphore()

    def greet(step, carry):
        peer = lax.rem(me + step, peers)
        pl.semaphore_signal(barrier, inc=1, device_id={"src": peer}, device_id_type=MESH)
        return carry

    lax.fori_loop(1, peers, greet, 0)
    for step in range(1, halves):
        other = lax.rem(my_half + step, halves)
        pl.semaphore_signal(barrier, inc=1, device_id={"tgt": other}, device_id_type=MESH)

    def row_copy(rounds, slot, other):
        return pltpu.make_async_remote_copy(
            src_ref=row_buf.at[rounds, slot],
            dst_ref=row_buf.at[rounds, slot],
            send_sem=row_send.at[rounds, other],
            recv_sem=row_recv.at[rounds, slot],
            device_id={"tgt": other},
            device_id_type=MESH,
        )

    def part_copy(rounds, slot, peer):
        return pltpu.make_async_remote_copy(
            src_ref=part_buf.at[rounds, peer],
            dst_ref=recv_buf.at[rounds, slot],
            send_sem=part_send.at[rounds, peer],
            recv_sem=part_recv.at[rounds, slot],
            device_id={"src": peer},
            device_id_type=MESH,
        )

    def pot_copy(rounds, slot, peer):
        return pltpu.make_async_remote_copy(
            src_ref=pot_buf.at[rounds, slot],
            dst_ref=pot_buf.at[rounds, slot],
            send_sem=pot_send.at[rounds, peer],
            recv_sem=pot_recv.at[rounds, slot],
            device_id={"src": peer},
            device_id_type=MESH,
        )

    line = lax.broadcasted_iota(jnp.int32, (width, width), 1)
    eye = lax.broadcasted_iota(jnp.int32, (width, width), 0) == line
    square = lax.broadcasted_iota(jnp.int32, (tiles, width), 1)
    across = lax.broadcasted_iota(jnp.int32, (tiles, tiles), 1)
    tile_eye = lax.broadcasted_iota(jnp.int32, (tiles, tiles), 0) == across

    def column(row, diagonal):
        spread = jnp.broadcast_to(row, diagonal.shape)
        return jnp.sum(jnp.where(diagonal, spread, 0.0), axis=1, keepdims=True)

    for load in loads:
        load.wait()

    xt = xt_ref[...].astype(jnp.float32)
    src_norm = 0.5 * jnp.sum(xt * xt, axis=0, keepdims=True)
    x_ref[...] = xt.T.astype(x_ref.dtype)

    tgt_count = column(tgt_count_ref[...].astype(jnp.float32), tile_eye)
    tgt_valid = square.astype(jnp.float32) < tgt_count
    logw = jnp.where(tgt_valid, tgt_logw_ref[...] * LOG2E, NEG)
    for a in range(clusters):
        flags = column(kept_ref[a : a + 1, :].astype(jnp.float32), tile_eye)
        closed = jnp.broadcast_to(jnp.where(flags > 0.5, 0.0, NEG), (tiles, width))
        base = logw + closed
        for p in range(peers):
            for h in range(groups):
                first = (p * groups + h) * size
                mask_ref[a, p, h] = closed[first : first + size]
                base_ref[a, p, h] = base[first : first + size]
    top_ref[...] = jnp.full(top_ref.shape, NEG, jnp.float32)
    sum_ref[...] = jnp.zeros(sum_ref.shape, jnp.float32)

    block = 16

    def absorb(p, h, potential):
        for a in range(clusters):
            added = base_ref[a, p, h] + potential
            for first in range(a * width, (a + 1) * width, block):
                scores = [
                    prod_ref[(p * groups + h) * size + k, pl.ds(first, block), :]
                    + jnp.broadcast_to(added[k : k + 1], (block, width))
                    for k in range(size)
                ]
                at = pl.ds(first, block)
                old = top_ref[at, :]
                top = jnp.maximum(old, tree(jnp.maximum, scores))
                total = tree(jnp.add, [jnp.exp2(score - top) for score in scores])
                sum_ref[at, :] = sum_ref[at, :] * jnp.exp2(old - top) + total
                top_ref[at, :] = top

    def first_rows(q, carry):
        p, h = q // groups, lax.rem(q, groups)
        load_targets(q).wait()
        yt = yt_ref[:, pl.ds(pl.multiple_of(q * span, span), span)]
        values = yt.astype(jnp.float32)
        norm = 0.5 * jnp.sum(values * values, axis=0, keepdims=True)
        for k in range(size):
            norm_ref[p, h, k : k + 1, :] = norm[:, k * width : (k + 1) * width]
        dots = lax.dot_general(
            x_ref[...], yt, (((1,), (0,)), ((), ())), preferred_element_type=jnp.float32
        )
        for k in range(size):
            prod_ref[q * size + k] = SCALE * dots[:, k * width : (k + 1) * width]
        absorb(p, h, SCALE * (g_init_ref[p, h] - norm_ref[p, h]))
        return carry

    def later_rows(rounds, p):
        for h in range(groups):
            absorb(p, h, pot_buf[rounds - 1, p, h])

    def columns(p, h):
        for k in range(size):
            tile = (p * groups + h) * size + k
            for a in range(clusters):
                scores = [
                    prod_ref[tile, pl.ds(first, 8), :] + bias_ref[pl.ds(first, 8), :]
                    for first in range(a * width, (a + 1) * width, 8)
                ]
                top = tree(jnp.maximum, scores)
                total = tree(jnp.add, [jnp.exp2(score - top) for score in scores])
                best = jnp.max(top, axis=0, keepdims=True)
                total = jnp.sum(total * jnp.exp2(top - best), axis=0, keepdims=True)
                col_top_ref[h, a, k : k + 1, :] = best
                col_sum_ref[h, a, k : k + 1, :] = total
        tops = [col_top_ref[h, a] + mask_ref[a, p, h] for a in range(clusters)]
        best = tree(jnp.maximum, tops)
        total = tree(
            jnp.add, [col_sum_ref[h, a] * jnp.exp2(tops[a] - best) for a in range(clusters)]
        )
        return best + log_two(total)

    for rounds in range(ITERS):
        if rounds == 0:
            lax.fori_loop(0, peers * groups, first_rows, 0)
            pl.semaphore_wait(barrier, peers - 1 + halves - 1)
        else:
            top_ref[...] = jnp.full(top_ref.shape, NEG, jnp.float32)
            sum_ref[...] = jnp.zeros(sum_ref.shape, jnp.float32)
            later_rows(rounds, me)

            def arrived(step, carry, rounds=rounds):
                p = partner(step)
                pot_copy(rounds - 1, p, p).wait_recv()
                later_rows(rounds, p)
                return carry

            lax.fori_loop(1, peers, arrived, 0)

        top = top_ref[...]
        best = jnp.max(top, axis=1, keepdims=True)
        total = jnp.sum(sum_ref[...] * jnp.exp2(top - best), axis=1, keepdims=True)
        level = jnp.broadcast_to(best + log_two(total), (rows, width))
        for a in range(clusters):
            own = jnp.where(eye, level[a * width : (a + 1) * width], 0.0)
            row_buf[rounds, my_half, a : a + 1, :] = jnp.sum(own, axis=0, keepdims=True)
        others = [lax.rem(my_half + step, halves) for step in range(1, halves)]
        for other in others:
            row_copy(rounds, my_half, other).start()
        for other in others:
            row_copy(rounds, other, other).wait_recv()
        levels = [row_buf[rounds, half] for half in range(halves)]
        best = tree(jnp.maximum, levels)
        total = tree(jnp.add, [jnp.exp2(level - best) for level in levels])
        src_pot = -(best + log_two(total))
        for a in range(clusters):
            live = line[:1] < src_count_ref[a]
            own = src_logw_ref[a : a + 1, :] * LOG2E + src_pot[a : a + 1]
            bias = column(jnp.where(live, own, NEG), eye)
            bias_ref[a * width : (a + 1) * width, :] = jnp.broadcast_to(bias, (width, width))

        def send_part(step, carry, rounds=rounds):
            p = partner(peers - step)
            for h in range(groups):
                part_buf[rounds, p, h] = columns(p, h)
            part_copy(rounds, me, p).start()
            return carry

        lax.fori_loop(1, peers, send_part, 0)
        for h in range(groups):
            recv_buf[rounds, me, h] = columns(me, h)

        def got_part(step, carry, rounds=rounds):
            p = lax.rem(me + step, peers)
            part_copy(rounds, p, p).wait_recv()
            return carry

        lax.fori_loop(1, peers, got_part, 0)
        levels = [recv_buf[rounds, p] for p in range(peers)]
        best = tree(jnp.maximum, levels)
        total = tree(jnp.add, [jnp.exp2(level - best) for level in levels])
        tgt_pot = -(best + log_two(total))
        if rounds == ITERS - 1:
            tgt_pot = tgt_pot * (1.0 / SCALE) + norm_ref[me]
        pot_buf[rounds, me] = tgt_pot

        def send_pot(step, carry, rounds=rounds):
            pot_copy(rounds, me, partner(peers - step)).start()
            return carry

        lax.fori_loop(1, peers, send_pot, 0)

    for a in range(clusters):
        norm = src_norm[:, a * width : (a + 1) * width]
        out_src_ref[a : a + 1, :] = src_pot[a : a + 1] * (1.0 / SCALE) + norm

    def got_pot(step, carry):
        p = lax.rem(me + step, peers)
        pot_copy(ITERS - 1, p, p).wait_recv()
        return carry

    lax.fori_loop(1, peers, got_pot, 0)
    out_tgt_ref[...] = pot_buf[ITERS - 1]

    for rounds in range(ITERS):
        for other in others:
            row_copy(rounds, my_half, other).wait_send()

        def sent(step, carry, rounds=rounds):
            p = lax.rem(me + step, peers)
            part_copy(rounds, me, p).wait_send()
            pot_copy(rounds, me, p).wait_send()
            return carry

        lax.fori_loop(1, peers, sent, 0)


def local(src_points, tgt_points, src_logw, tgt_logw, src_count, tgt_count, kept, g_init):
    rows, feature = src_points.shape
    tgt_rows = tgt_points.shape[0]
    clusters = src_count.shape[0]
    tiles = tgt_count.shape[0]
    width = rows // clusters
    peers = lax.axis_size("src")
    halves = lax.axis_size("tgt")
    share = tiles // peers
    size = math.gcd(share, 8)
    groups = share // size
    dims = (clusters, tiles, width, peers, halves, groups, size)
    cut = (peers, groups, size, width)
    f32 = jnp.float32
    vmem = pl.BlockSpec(memory_space=pltpu.VMEM)
    hbm = pl.BlockSpec(memory_space=pltpu.HBM)
    dma = pltpu.SemaphoreType.DMA
    src_pot, tgt_pot = pl.pallas_call(
        functools.partial(kernel, dims),
        out_shape=(jax.ShapeDtypeStruct((clusters, width), f32), jax.ShapeDtypeStruct(cut, f32)),
        in_specs=[hbm] * 8,
        out_specs=(vmem, vmem),
        scratch_shapes=[
            pltpu.VMEM((feature, rows), src_points.dtype),
            pltpu.VMEM((feature, tgt_rows), tgt_points.dtype),
            pltpu.VMEM((clusters, width), f32),
            pltpu.VMEM((tiles, width), f32),
            pltpu.SMEM((clusters,), jnp.int32),
            pltpu.VMEM((1, tiles), jnp.int32),
            pltpu.VMEM((clusters, tiles), jnp.int32),
            pltpu.VMEM(cut, f32),
            dma((7,)),
            dma((peers * groups,)),
            pltpu.VMEM((rows, feature), src_points.dtype),
            pltpu.VMEM((tiles, rows, width), f32),
            pltpu.VMEM((clusters,) + cut, f32),
            pltpu.VMEM((clusters,) + cut, f32),
            pltpu.VMEM(cut, f32),
            pltpu.VMEM((rows, width), f32),
            pltpu.VMEM((rows, width), f32),
            pltpu.VMEM((rows, width), f32),
            pltpu.VMEM((groups, clusters, size, width), f32),
            pltpu.VMEM((groups, clusters, size, width), f32),
            pltpu.VMEM((ITERS, halves, clusters, width), f32),
            pltpu.VMEM((ITERS,) + cut, f32),
            pltpu.VMEM((ITERS,) + cut, f32),
            pltpu.VMEM((ITERS,) + cut, f32),
            dma((ITERS, halves)),
            dma((ITERS, halves)),
            dma((ITERS, peers)),
            dma((ITERS, peers)),
            dma((ITERS, peers)),
            dma((ITERS, peers)),
        ],
        compiler_params=pltpu.CompilerParams(
            collective_id=0, has_side_effects=True, vmem_limit_bytes=60 * 1024 * 1024
        ),
    )(
        src_points.T,
        tgt_points.T,
        src_logw.reshape(clusters, width),
        tgt_logw.reshape(tiles, width),
        src_count,
        tgt_count.reshape(1, tiles),
        kept,
        g_init.reshape(cut),
    )
    return (src_pot.reshape(rows), tgt_pot.reshape(tgt_rows))


def solution(mesh):
    return jax.shard_map(
        local,
        mesh=mesh,
        in_specs=(
            P(("grp", "src"), None),
            P(("grp", "tgt"), None),
            P(("grp", "src")),
            P(("grp", "tgt")),
            P(("grp", "src")),
            P(("grp", "tgt")),
            P(("grp", "src"), "tgt"),
            P(("grp", "tgt")),
        ),
        out_specs=(P(("grp", "src")), P(("grp", "tgt"))),
        check_vma=False,
    )
```
